32 devices in a mesh: row: 8 (over y, x, core), col: 4 (over z).
Axes of the slice: x: 2, y: 2, z: 4, core: 2. Of those that a mesh axis runs over, the one named last changes fastest.
Arguments:
- near_blocks: float32 [8, 16, 512, 512], P('row', 'col'), as said below
- leaf_bases: float32 [8, 512, 512], P('row'), may hold values from -1 to 1, as said below
- upper_bases: float32 [4, 256, 256], P('col'), may hold values from -1 to 1, as said below
- near_list: int32 [8, 16], P('row'), may hold values from 0 to 7, as said below
Outputs:
- factors: float32 [3072, 384], P('row')
- skeleton: float32 [1024, 1024], P('row', 'col')
- upper_skeleton: float32 [512, 512], P('row', 'col')
The draws below stay inside these ranges and needn't reach their ends.
Inputs may be any that keep to these rules, and one draw needn't show every extreme that they name: `near_list`: entry 0 of row i is i; every entry of row i lies within 2 of i; entries may repeat. near_blocks[i, k] is the tile between leaf i and leaf near_list[i, k] of a symmetric matrix: a kernel matrix of points, a positive diagonal noise term and independent symmetric random entries; entries naming the same leaf hold equal tiles; every diagonal tile is symmetric positive definite. Each leaf_bases[i] is orthogonal. Each upper_bases[p] is orthogonal.
All inputs are finite; a program needn't handle non-finite values.
Results may differ from the reference program's by a relative error of at most 0.0003.
Values sent between devices are 32-bit elements; how exact they have to be, the bound alone decides.
A program may use at most 64 MiB of HBM per device.

```python
import math
import jax
import jax.numpy as jnp
from jax import lax

LEAF = 512
SKEL = 128
NEAR = 16
REACH = 2
RED = 384
LEAVES = 8
PARENTS = 4
PARENT = 256


noise_level = 0.015


def orthonormal(key, count, order):
    source = jax.random.normal(key, (count, order, order), jnp.float32)
    ortho, triangle = jnp.linalg.qr(source)
    return ortho


def near_lists(key):
    own_index = jnp.arange(LEAVES, dtype=jnp.int32)[:, None]
    offsets = jax.random.randint(jax.random.fold_in(key, 37), (LEAVES, NEAR), -REACH, REACH + 1)
    listed = jnp.clip(own_index + offsets, 0, LEAVES - 1).astype(jnp.int32)
    column = jnp.arange(NEAR, dtype=jnp.int32)[None, :]
    return jnp.where(column == 0, own_index, listed).astype(jnp.int32)


def leaf_points(key):
    uniforms = jax.random.uniform(jax.random.fold_in(key, 53), (LEAVES, LEAF, 3), jnp.float32)
    across = uniforms[:, :, 0]
    first_coord = jnp.arange(LEAVES, dtype=jnp.float32)[:, None] + across
    return jnp.stack([first_coord, 2.0 * uniforms[:, :, 1], 2.0 * uniforms[:, :, 2]], axis=-1)


def pair_entries(pair_key):
    return jax.random.normal(pair_key, (LEAF, LEAF), jnp.float32)


def symmetric_noise(noise_base, leaf, other):
    forward = pair_entries(jax.random.fold_in(noise_base, leaf * LEAVES + other))
    backward = pair_entries(jax.random.fold_in(noise_base, other * LEAVES + leaf))
    return noise_level / math.sqrt(2.0) * (forward + backward.T)


def draw_near_blocks(key, part):
    listed = near_lists(key)
    points = leaf_points(key)
    noise_key = jax.random.fold_in(key, 61)
    entry_key = jax.random.fold_in(key, 71)
    ridge = jnp.exp(jax.random.uniform(noise_key, (LEAVES, LEAF), jnp.float32, math.log(2.0), math.log(6.0)))
    kernel_scale = 6.0 / LEAF

    def one_leaf(leaf):
        own_points = points[leaf]
        near_points = points[listed[leaf]]
        offsets = own_points[None, :, None, :] - near_points[:, None, :, :]
        distance = jnp.sqrt(jnp.sum(offsets * offsets, axis=-1))
        tiles = kernel_scale * jnp.exp(-distance)
        random_part = jax.vmap(lambda other: symmetric_noise(entry_key, leaf, other))(listed[leaf])
        same_leaf = (listed[leaf] == leaf)[:, None, None]
        return tiles + random_part + jnp.where(same_leaf, jnp.diag(ridge[leaf])[None, :, :], 0.0)
    return lax.map(one_leaf, jnp.arange(LEAVES, dtype=jnp.int32)).astype(jnp.float32)


def draw_leaf_bases(key, part):
    return orthonormal(jax.random.fold_in(key, 11), LEAVES, LEAF)


def draw_upper_bases(key, part):
    return orthonormal(jax.random.fold_in(key, 23), PARENTS, PARENT)


def draw_near_list(key, part):
    return near_lists(key)


def setup_inputs(seed: int = 0) -> dict:
    arg_keys = jax.random.split(jax.random.key(seed), 5)
    near_blocks = draw_near_blocks(jax.random.fold_in(arg_keys[4], 71), 0)
    leaf_bases = draw_leaf_bases(jax.random.fold_in(arg_keys[4], 71), 0)
    upper_bases = draw_upper_bases(jax.random.fold_in(arg_keys[4], 71), 0)
    near_list = draw_near_list(jax.random.fold_in(arg_keys[4], 71), 0)
    return {"near_blocks": near_blocks, "leaf_bases": leaf_bases, "upper_bases": upper_bases, "near_list": near_list}


def product(left, right):
    return jnp.dot(left, right, precision=lax.Precision.HIGHEST)

def lower_solve(factor, rhs):
    return lax.linalg.triangular_solve(factor, rhs, left_side=True, lower=True)

def reference(near_blocks, leaf_bases, upper_bases, near_list):
    leaves = jnp.arange(LEAVES, dtype=jnp.int32)

    def leaf_pivot(col_leaf):
        leaf_basis = leaf_bases[col_leaf]
        rotated = product(product(leaf_basis.T, near_blocks[col_leaf, 0]), leaf_basis)
        factor = jnp.linalg.cholesky(rotated[:RED, :RED])
        return (factor, lower_solve(factor, rotated[:RED, RED:]))
    factor_all, coupling_all = lax.map(leaf_pivot, leaves)

    def leaf_block(row_leaf, col_leaf):
        matches = near_list[row_leaf] == col_leaf
        first_match = jnp.argmax(matches).astype(jnp.int32)

        def live_block(operand):
            near_tile = near_blocks[row_leaf, first_match]
            skel_rows = product(leaf_bases[row_leaf][:, RED:].T, near_tile)
            rotated = product(skel_rows, leaf_bases[col_leaf])
            solved = lower_solve(factor_all[col_leaf], rotated[:, :RED].T)
            return rotated[:, RED:] - product(solved.T, coupling_all[col_leaf])

        def empty_block(operand):
            return jnp.zeros((SKEL, SKEL), jnp.float32)
        return lax.cond(jnp.any(matches), live_block, empty_block, 0)

    def leaf_row(row_leaf):
        return lax.map(lambda col_leaf: leaf_block(row_leaf, col_leaf), leaves)
    blocks = lax.map(leaf_row, leaves)
    skeleton = blocks.transpose(0, 2, 1, 3).reshape(LEAVES * SKEL, LEAVES * SKEL)
    parents = jnp.arange(PARENTS, dtype=jnp.int32)

    def parent_rotated(row_parent, col_parent):
        merged = lax.dynamic_slice(skeleton, (row_parent * PARENT, col_parent * PARENT), (PARENT, PARENT))
        return product(product(upper_bases[row_parent].T, merged), upper_bases[col_parent])

    def parent_pivot(col_parent):
        rotated = parent_rotated(col_parent, col_parent)
        factor = jnp.linalg.cholesky(rotated[:SKEL, :SKEL])
        return (factor, lower_solve(factor, rotated[:SKEL, SKEL:]))
    parent_factors, parent_couplings = lax.map(parent_pivot, parents)

    def parent_block(row_parent, col_parent):
        rotated = parent_rotated(row_parent, col_parent)
        solved = lower_solve(parent_factors[col_parent], rotated[SKEL:, :SKEL].T)
        return rotated[SKEL:, SKEL:] - product(solved.T, parent_couplings[col_parent])

    def parent_row(row_parent):
        return lax.map(lambda col_parent: parent_block(row_parent, col_parent), parents)
    upper_blocks = lax.map(parent_row, parents)
    upper_skeleton = upper_blocks.transpose(0, 2, 1, 3).reshape(PARENTS * SKEL, PARENTS * SKEL)
    return (factor_all.reshape(LEAVES * RED, RED), skeleton, upper_skeleton)
```

```python
import functools

import jax
import jax.numpy as jnp
from jax import lax
from jax.experimental import pallas as pl
from jax.experimental.pallas import tpu as pltpu
from jax.sharding import PartitionSpec as P

SKEL = 128
REACH = 2
BLK = 128
PANEL = 8
F32 = jnp.float32
BF16 = jnp.bfloat16


def split(x):
    hi = x.astype(BF16)
    lo = (x - hi.astype(F32)).astype(BF16)
    return hi, lo


def mm(left, right, dims):
    lh, ll = split(left)
    rh, rl = split(right)
    dot = functools.partial(
        lax.dot_general, dimension_numbers=(dims, ((), ())), preferred_element_type=F32
    )
    return dot(lh, rh) + (dot(lh, rl) + dot(ll, rh))


NN = ((1,), (0,))
TN = ((0,), (0,))
NT = ((1,), (1,))


def panel_step(rows, base):
    width = rows.shape[1]
    sub = lax.broadcasted_iota(jnp.int32, (PANEL, 128), 0)
    cols = [
        jnp.broadcast_to(rows[:, base + t : base + t + 1], (PANEL, 128)) for t in range(PANEL)
    ]
    parts = [rows[:, c : c + 128] for c in range(0, width, 128)]
    for t in range(PANEL):
        scale = lax.rsqrt(cols[t][t : t + 1, :])
        mult = jnp.where(sub > t, cols[t] * scale, 0.0)
        for u in range(t + 1, PANEL):
            cols[u] = cols[u] - mult * (cols[u][t : t + 1, :] * scale)
        for c in range(len(parts)):
            lead = parts[c][t : t + 1, :] * scale
            parts[c] = jnp.where(sub == t, lead, parts[c] - mult * lead)
    return jnp.concatenate(parts, axis=1)


def chol_inv(work):
    for base in range(0, BLK, PANEL):
        rows = panel_step(work[base : base + PANEL, :], base)
        work[base : base + PANEL, :] = rows
        rest = BLK - base - PANEL
        if rest:
            high = rows.astype(BF16).astype(F32)
            low = rows - high
            left = jnp.concatenate([high, high, low, low], axis=0)[:, :BLK].astype(BF16)
            right = jnp.concatenate([high, low, high, low], axis=0).astype(BF16)
            update = lax.dot_general(
                left, right, (TN, ((), ())), preferred_element_type=F32
            )
            work[base + PANEL :, :] = work[base + PANEL :, :] - update[base + PANEL :, :]


def load_block(work, block):
    row = lax.broadcasted_iota(jnp.int32, (BLK, BLK), 0)
    col = lax.broadcasted_iota(jnp.int32, (BLK, BLK), 1)
    work[:, :BLK] = (block + block.T) * 0.5
    work[:, BLK:] = jnp.where(row == col, 1.0, 0.0)


def upper_part(block):
    row = lax.broadcasted_iota(jnp.int32, (BLK, BLK), 0)
    col = lax.broadcasted_iota(jnp.int32, (BLK, BLK), 1)
    return jnp.where(col >= row, block, 0.0)


def pivot_kernel(near_ref, basis_ref, factor_ref, combined_ref, mat, work):
    order = basis_ref.shape[0]
    red = order - SKEL
    count = red // BLK
    rotated = mm(basis_ref[:, :red], mm(near_ref[...], basis_ref[...], NN), TN)
    square = rotated[:, :red]
    mat[:, :red] = (square + square.T) * 0.5
    mat[:, red:] = rotated[:, red:]
    factor_ref[...] = jnp.zeros_like(factor_ref)
    inverses, leads = [], []
    for j in range(count):
        lo, hi = j * BLK, (j + 1) * BLK
        load_block(work, mat[lo:hi, lo:hi])
        chol_inv(work)
        factor_ref[lo:hi, lo:hi] = upper_part(work[:, :BLK]).T
        inverse = work[:, BLK:]
        lead = mm(inverse, mat[lo:hi, hi:], NN)
        if hi < red:
            factor_ref[hi:red, lo:hi] = lead[:, : red - hi].T
            mat[hi:red, hi:] = mat[hi:red, hi:] - mm(lead[:, : red - hi], lead, TN)
        inverses.append(inverse)
        leads.append(lead)
    folded = []
    for j in reversed(range(count)):
        rest = red - (j + 1) * BLK
        rhs = leads[j][:, rest:]
        if folded:
            rhs = rhs - mm(leads[j][:, :rest], jnp.concatenate(folded, axis=0), NN)
        folded.insert(0, mm(inverses[j], rhs, TN))
    combined_ref[...] = basis_ref[:, red:] - mm(
        basis_ref[:, :red], jnp.concatenate(folded, axis=0), NN
    )


def pivot(near_tile, basis):
    order = basis.shape[0]
    red = order - SKEL
    return pl.pallas_call(
        pivot_kernel,
        out_shape=(
            jax.ShapeDtypeStruct((red, red), F32),
            jax.ShapeDtypeStruct((order, SKEL), F32),
        ),
        in_specs=[pl.BlockSpec(memory_space=pltpu.VMEM)] * 2,
        out_specs=[pl.BlockSpec(memory_space=pltpu.VMEM)] * 2,
        scratch_shapes=[pltpu.VMEM((red, order), F32), pltpu.VMEM((BLK, 2 * BLK), F32)],
        compiler_params=pltpu.CompilerParams(vmem_limit_bytes=32 * 1024 * 1024),
        name="leaf_pivot",
    )(near_tile, basis)


def fold_kernel(rotated_ref, out_ref, work):
    load_block(work, rotated_ref[:SKEL, :SKEL])
    chol_inv(work)
    inverse = work[:, BLK:]
    out_ref[...] = mm(inverse, mm(inverse, rotated_ref[:SKEL, SKEL:], NN), TN)


def fold(rotated):
    return pl.pallas_call(
        fold_kernel,
        out_shape=jax.ShapeDtypeStruct((SKEL, SKEL), F32),
        in_specs=[pl.BlockSpec(memory_space=pltpu.VMEM)],
        out_specs=pl.BlockSpec(memory_space=pltpu.VMEM),
        scratch_shapes=[pltpu.VMEM((BLK, 2 * BLK), F32)],
        name="parent_pivot",
    )(rotated)


def spread(block, axis):
    step = lax.axis_size(axis) // 2
    index = lax.axis_index(axis)
    while step >= 1:
        pairs = [(i, i + step) for i in range(0, lax.axis_size(axis), 2 * step)]
        got = lax.ppermute(block, axis, pairs)
        block = jnp.where(index % (2 * step) == step, got, block)
        step //= 2
    return block


def from_behind(block, axis, distance):
    devices = range(lax.axis_size(axis))
    route = [(i - distance, i) for i in devices if i - distance in devices]
    return lax.ppermute(block, axis, route)


def swapped(value, axis, distance):
    mask = 2**distance
    pairs = [(source, source ^ mask) for source in range(lax.axis_size(axis))]
    return lax.ppermute(value, axis, pairs)


def product(left, right):
    return jnp.dot(left, right, precision=lax.Precision.HIGH)


def local(near_blocks, leaf_bases, upper_bases, near_list):
    leaf_order = leaf_bases.shape[1]
    red_count = leaf_order - SKEL
    entry_count = near_blocks.shape[1]
    row_index = lax.axis_index("row")
    col_index = lax.axis_index("col")
    row_slot = row_index % 2
    holder = row_index // 2
    own_basis = leaf_bases[0]
    near_row = near_list[0]
    parent_reach = (REACH + 1) // 2

    def blank_pivot(near_tile, basis):
        return (
            jnp.zeros((red_count, red_count), F32),
            jnp.zeros((leaf_order, SKEL), F32),
        )

    factor, combined = lax.cond(
        col_index == 0, pivot, blank_pivot, near_blocks[0, 0], own_basis
    )
    combined = spread(combined, "col")
    factor = spread(factor, "col")
    skel_basis_t = own_basis[:, red_count:].T
    row_products = []
    slot_list = []
    for entry in range(entry_count):
        row_products.append(product(skel_basis_t, near_blocks[0, entry]))
        col_leaf = lax.dynamic_index_in_dim(
            near_row, col_index * entry_count + entry, 0, keepdims=False
        )
        slot_list.append(col_leaf - row_index + REACH)
    tile_list = []
    combined_list = []
    for offset in range(-REACH, REACH + 1):
        if offset == 0:
            combined_list.append(combined)
        else:
            combined_list.append(from_behind(combined, "row", -offset))
    combined_table = jnp.stack(combined_list)
    for entry in range(entry_count):
        column_part = lax.dynamic_index_in_dim(combined_table, slot_list[entry], 0, keepdims=False)
        tile_list.append(product(row_products[entry], column_part))
    compact = jnp.stack(tile_list)
    gathered = lax.all_gather(compact, "col", axis=0, tiled=True)
    strips = []
    for column_slot in range(2):
        target_leaf = col_index * 2 + column_slot
        matches = near_row == target_leaf
        first_match = jnp.argmax(matches)
        picked = lax.dynamic_index_in_dim(gathered, first_match, 0, keepdims=False)
        strips.append(jnp.where(jnp.any(matches), picked, jnp.zeros_like(picked)))
    skeleton_strip = jnp.concatenate(strips, axis=1)
    partner = swapped(skeleton_strip, "row", 0)
    merged = jnp.where(
        row_slot == 0,
        jnp.concatenate([skeleton_strip, partner], axis=0),
        jnp.concatenate([partner, skeleton_strip], axis=0),
    )
    upper_basis = upper_bases[0]
    basis_pieces = []
    for offset in range(-parent_reach, parent_reach + 1):
        if offset == 0:
            basis_pieces.append(upper_basis)
        else:
            basis_pieces.append(from_behind(upper_basis, "col", -offset))
    parent_table = jnp.stack(basis_pieces)
    basis_slot = jnp.clip(holder - col_index + parent_reach, 0, 2 * parent_reach)
    parent_basis = lax.dynamic_index_in_dim(parent_table, basis_slot, 0, keepdims=False)
    parent_rotated = product(parent_basis.T, product(merged, upper_basis))
    folded = lax.cond(
        row_index == col_index * 2, fold, lambda block: jnp.zeros((SKEL, SKEL), F32), parent_rotated
    )
    pieces = []
    for offset in range(-2 * parent_reach - 1, 2 * parent_reach + 1):
        pieces.append(folded if offset == 0 else from_behind(folded, "row", -offset))
    pivot_slot = jnp.clip(2 * col_index - row_index + 2 * parent_reach + 1, 0, 4 * parent_reach + 1)
    chosen = lax.dynamic_index_in_dim(jnp.stack(pieces), pivot_slot, 0, keepdims=False)
    in_window = jnp.abs(holder - col_index) <= parent_reach
    chosen = jnp.where(in_window, chosen, jnp.zeros_like(chosen))
    low_rows = lax.dynamic_slice_in_dim(
        parent_rotated, SKEL + row_slot * (SKEL // 2), SKEL // 2, 0
    )
    upper_half = low_rows[:, SKEL:] - product(low_rows[:, :SKEL], chosen)
    return (factor, skeleton_strip, upper_half)


def solution(mesh):
    return jax.shard_map(
        local,
        mesh=mesh,
        in_specs=(
            P("row", "col", None, None),
            P("row", None, None),
            P("col", None, None),
            P("row", None),
        ),
        out_specs=(P("row", None), P("row", "col"), P("row", "col")),
        check_vma=False,
    )
```

```python
import functools

import jax
import jax.numpy as jnp
from jax import lax
from jax.experimental import pallas as pl
from jax.experimental.pallas import tpu as pltpu
from jax.sharding import PartitionSpec as P

SKEL = 128
REACH = 2
BLK = 128
PANEL = 8
CHUNKS = 2
F32 = jnp.float32
BF16 = jnp.bfloat16


def split(x):
    hi = x.astype(BF16)
    lo = (x - hi.astype(F32)).astype(BF16)
    return hi, lo


def mm(left, right, dims):
    lh, ll = split(left)
    rh, rl = split(right)
    dot = functools.partial(
        lax.dot_general, dimension_numbers=(dims, ((), ())), preferred_element_type=F32
    )
    return dot(lh, rh) + (dot(lh, rl) + dot(ll, rh))


NN = ((1,), (0,))
TN = ((0,), (0,))
NT = ((1,), (1,))


def panel_step(rows, base):
    width = rows.shape[1]
    sub = lax.broadcasted_iota(jnp.int32, (PANEL, 128), 0)
    cols = [
        jnp.broadcast_to(rows[:, base + t : base + t + 1], (PANEL, 128)) for t in range(PANEL)
    ]
    parts = [rows[:, c : c + 128] for c in range(0, width, 128)]
    for t in range(PANEL):
        scale = lax.rsqrt(cols[t][t : t + 1, :])
        mult = jnp.where(sub > t, cols[t] * scale, 0.0)
        for u in range(t + 1, PANEL):
            cols[u] = cols[u] - mult * (cols[u][t : t + 1, :] * scale)
        for c in range(len(parts)):
            lead = parts[c][t : t + 1, :] * scale
            parts[c] = jnp.where(sub == t, lead, parts[c] - mult * lead)
    return jnp.concatenate(parts, axis=1)


def chol_inv(work):
    for base in range(0, BLK, PANEL):
        rows = panel_step(work[base : base + PANEL, :], base)
        work[base : base + PANEL, :] = rows
        rest = BLK - base - PANEL
        if rest:
            high = rows.astype(BF16).astype(F32)
            low = rows - high
            left = jnp.concatenate([high, high, low, low], axis=0)[:, :BLK].astype(BF16)
            right = jnp.concatenate([high, low, high, low], axis=0).astype(BF16)
            update = lax.dot_general(
                left, right, (TN, ((), ())), preferred_element_type=F32
            )
            work[base + PANEL :, :] = work[base + PANEL :, :] - update[base + PANEL :, :]


def load_block(work, block):
    row = lax.broadcasted_iota(jnp.int32, (BLK, BLK), 0)
    col = lax.broadcasted_iota(jnp.int32, (BLK, BLK), 1)
    work[:, :BLK] = (block + block.T) * 0.5
    work[:, BLK:] = jnp.where(row == col, 1.0, 0.0)


def upper_part(block):
    row = lax.broadcasted_iota(jnp.int32, (BLK, BLK), 0)
    col = lax.broadcasted_iota(jnp.int32, (BLK, BLK), 1)
    return jnp.where(col >= row, block, 0.0)


def pivot_kernel(near_ref, basis_ref, factor_ref, combined_ref, mat, work):
    order = basis_ref.shape[0]
    red = order - SKEL
    count = red // BLK
    rotated = mm(basis_ref[:, :red], mm(near_ref[...], basis_ref[...], NN), TN)
    square = rotated[:, :red]
    mat[:, :red] = (square + square.T) * 0.5
    mat[:, red:] = rotated[:, red:]
    factor_ref[...] = jnp.zeros_like(factor_ref)
    inverses, leads = [], []
    for j in range(count):
        lo, hi = j * BLK, (j + 1) * BLK
        load_block(work, mat[lo:hi, lo:hi])
        chol_inv(work)
        factor_ref[lo:hi, lo:hi] = upper_part(work[:, :BLK]).T
        inverse = work[:, BLK:]
        lead = mm(inverse, mat[lo:hi, hi:], NN)
        if hi < red:
            factor_ref[hi:red, lo:hi] = lead[:, : red - hi].T
            mat[hi:red, hi:] = mat[hi:red, hi:] - mm(lead[:, : red - hi], lead, TN)
        inverses.append(inverse)
        leads.append(lead)
    folded = []
    for j in reversed(range(count)):
        rest = red - (j + 1) * BLK
        rhs = leads[j][:, rest:]
        if folded:
            rhs = rhs - mm(leads[j][:, :rest], jnp.concatenate(folded, axis=0), NN)
        folded.insert(0, mm(inverses[j], rhs, TN))
    combined_ref[...] = basis_ref[:, red:] - mm(
        basis_ref[:, :red], jnp.concatenate(folded, axis=0), NN
    )


def pivot(near_tile, basis):
    order = basis.shape[0]
    red = order - SKEL
    return pl.pallas_call(
        pivot_kernel,
        out_shape=(
            jax.ShapeDtypeStruct((red, red), F32),
            jax.ShapeDtypeStruct((order, SKEL), F32),
        ),
        in_specs=[pl.BlockSpec(memory_space=pltpu.VMEM)] * 2,
        out_specs=[pl.BlockSpec(memory_space=pltpu.VMEM)] * 2,
        scratch_shapes=[pltpu.VMEM((red, order), F32), pltpu.VMEM((BLK, 2 * BLK), F32)],
        compiler_params=pltpu.CompilerParams(vmem_limit_bytes=32 * 1024 * 1024),
        name="leaf_pivot",
    )(near_tile, basis)


def exchange_kernel(
    rows, cols, slot_ref, pick_ref, near_ref, skel_ref, combined_ref, factor_in,
    factor_ref, merged_ref, diag_ref, strip_ref,
    table, products, outgoing, incoming,
    chain_send, chain_recv, row_send, row_recv, fact_send, fact_recv,
    tile_send, tile_recv, pair_send, pair_recv, diag_send, diag_recv,
):
    row = lax.axis_index("row")
    col = lax.axis_index("col")
    entries = near_ref.shape[0]
    order = combined_ref.shape[0]
    red = order - SKEL
    step = order // CHUNKS
    reach_rows = 2 * ((REACH + 1) // 2) + 1
    holder = row // 2
    parity = row % 2
    parent_reach = (REACH + 1) // 2

    def remote(src, dst, send, recv, r, c):
        return pltpu.make_async_remote_copy(
            src_ref=src, dst_ref=dst, send_sem=send, recv_sem=recv,
            device_id=(r, c), device_id_type=pl.DeviceIdType.MESH,
        )

    table[...] = jnp.zeros_like(table)
    diag_ref[...] = jnp.zeros_like(diag_ref)
    for lo in range(0, red - BLK, BLK):
        factor_ref[lo : lo + BLK, lo + BLK :] = jnp.zeros((BLK, red - lo - BLK), F32)

    barrier = pltpu.get_barrier_semaphore()
    for d in range(-reach_rows, reach_rows + 1):
        if d:
            pl.semaphore_signal(
                barrier, inc=1, device_id=(lax.rem(row + d + rows, rows), col),
                device_id_type=pl.DeviceIdType.MESH,
            )
    for d in range(1, cols):
        pl.semaphore_signal(
            barrier, inc=1, device_id=(row, lax.rem(col + d, cols)),
            device_id_type=pl.DeviceIdType.MESH,
        )
    pl.semaphore_wait(barrier, 2 * reach_rows + cols - 1)

    @pl.when(col == 0)
    def _():
        table[REACH] = combined_ref[...]

    def chunk(slot, k):
        return table.at[slot, pl.ds(k * step, step), :]

    def chain(k):
        return remote(
            chunk(REACH, k), chunk(REACH, k), chain_send.at[k], chain_recv.at[k], row,
            lax.rem(col + 1, cols),
        )

    def to_row(d, k):
        return remote(
            chunk(REACH, k), chunk(REACH - d, k), row_send.at[d + REACH, k],
            row_recv.at[REACH - d, k], lax.rem(row + d + rows, rows), col,
        )

    offsets = [d for d in range(-REACH, REACH + 1) if d]
    for k in range(CHUNKS):
        @pl.when(col > 0)
        def _():
            chain(k).wait_recv()

        @pl.when(col < cols - 1)
        def _():
            chain(k).start()

        for d in offsets:
            @pl.when((row + d >= 0) & (row + d < rows))
            def _():
                to_row(d, k).start()

    def strip(j):
        return factor_ref.at[pl.ds(j * BLK, BLK), pl.ds(0, (j + 1) * BLK)]

    def send_factor(d, j):
        return remote(strip(j), strip(j), fact_send.at[d, j], fact_recv.at[j], row, d)

    @pl.when(col == 0)
    def _():
        factor_ref[...] = factor_in[...]
        for d in range(1, cols):
            for j in range(red // BLK):
                send_factor(d, j).start()

    for e in range(entries):
        products[e] = mm(skel_ref[...], near_ref[e], TN)

    for k in range(CHUNKS):
        for d in offsets:
            @pl.when((row + d >= 0) & (row + d < rows))
            def _():
                to_row(-d, k).wait_recv()

    tiles = [mm(products[e], table[slot_ref[e]], NN) for e in range(entries)]
    zero = jnp.zeros((SKEL, SKEL), F32)
    for t in range(2 * cols):
        total = zero
        for e in range(entries):
            total = total + jnp.where(pick_ref[t * entries + e] > 0, tiles[e], zero)
        outgoing[t // 2, :, (t % 2) * SKEL : (t % 2 + 1) * SKEL] = total

    def send_tile(d):
        other = lax.rem(col + d, cols)
        return remote(
            outgoing.at[other], incoming.at[d], tile_send.at[d], tile_recv.at[d], row, other
        )

    for d in range(1, cols):
        send_tile(d).start()
    total = outgoing[col]
    for d in range(1, cols):
        send_tile(d).wait_recv()
        total = total + incoming[d]
    strip_ref[...] = total
    merged_ref[parity] = total

    to_pair = remote(
        strip_ref, merged_ref.at[parity], pair_send, pair_recv, row + 1 - 2 * parity, col
    )
    to_pair.start()

    def to_diag(d):
        return remote(
            strip_ref, diag_ref.at[parity], diag_send.at[d + reach_rows],
            diag_recv.at[parity], lax.rem(row + d + rows, rows), col,
        )

    def sends_diag(d):
        other = row + d
        near = ((other + 2 * parent_reach) // 2 >= col) & (other // 2 <= col + parent_reach)
        return (holder == col) & (other >= 0) & (other < rows) & near

    @pl.when(holder == col)
    def _():
        diag_ref[parity] = total

    for d in range(-reach_rows, reach_rows + 1):
        if d:
            @pl.when(sends_diag(d))
            def _():
                to_diag(d).start()

    remote(
        strip_ref, merged_ref.at[1 - parity], pair_send, pair_recv, row + 1 - 2 * parity, col
    ).wait_recv()
    inside = (holder + parent_reach >= col) & (holder <= col + parent_reach)
    for s in range(2):
        @pl.when(inside & (row - 2 * col - s != 0))
        def _():
            remote(
                strip_ref, diag_ref.at[s], diag_send.at[0], diag_recv.at[s],
                row + 1 - 2 * parity, col,
            ).wait_recv()

    @pl.when(col > 0)
    def _():
        for j in range(red // BLK):
            send_factor(0, j).wait_recv()

    to_pair.wait_send()
    for d in range(-reach_rows, reach_rows + 1):
        if d:
            @pl.when(sends_diag(d))
            def _():
                to_diag(d).wait_send()
    for d in range(1, cols):
        send_tile(d).wait_send()
    for k in range(CHUNKS):
        @pl.when(col < cols - 1)
        def _():
            chain(k).wait_send()

        for d in offsets:
            @pl.when((row + d >= 0) & (row + d < rows))
            def _():
                to_row(d, k).wait_send()

    @pl.when(col == 0)
    def _():
        for d in range(1, cols):
            for j in range(red // BLK):
                send_factor(d, j).wait_send()


def exchange(slots, picks, near, skel_basis, combined, factor):
    rows, cols = lax.axis_size("row"), lax.axis_size("col")
    order = combined.shape[0]
    red = factor.shape[0]
    entries = near.shape[0]
    reach_rows = 2 * ((REACH + 1) // 2) + 1
    spans = 2 * REACH + 1
    vmem = pl.BlockSpec(memory_space=pltpu.VMEM)
    smem = pl.BlockSpec(memory_space=pltpu.SMEM)
    dma = pltpu.SemaphoreType.DMA
    return pl.pallas_call(
        functools.partial(exchange_kernel, rows, cols),
        out_shape=(
            jax.ShapeDtypeStruct((red, red), F32),
            jax.ShapeDtypeStruct((2, SKEL, 2 * SKEL), F32),
            jax.ShapeDtypeStruct((2, SKEL, 2 * SKEL), F32),
            jax.ShapeDtypeStruct((SKEL, 2 * SKEL), F32),
        ),
        in_specs=[smem, smem, vmem, vmem, vmem, vmem],
        out_specs=[vmem] * 4,
        scratch_shapes=[
            pltpu.VMEM((spans, order, SKEL), F32),
            pltpu.VMEM((entries, SKEL, order), F32),
            pltpu.VMEM((cols, SKEL, 2 * SKEL), F32),
            pltpu.VMEM((cols, SKEL, 2 * SKEL), F32),
            dma((CHUNKS,)), dma((CHUNKS,)),
            dma((spans, CHUNKS)), dma((spans, CHUNKS)),
            dma((cols, red // BLK)), dma((red // BLK,)),
            dma((cols,)), dma((cols,)),
            dma, dma,
            dma((2 * reach_rows + 1,)), dma((2,)),
        ],
        compiler_params=pltpu.CompilerParams(
            collective_id=0, has_side_effects=True, vmem_limit_bytes=40 * 1024 * 1024
        ),
        name="exchange",
    )(slots, picks, near, skel_basis, combined, factor)


def parent_kernel(merged_ref, diag_ref, row_basis, col_basis, out_ref, work):
    basis = col_basis[...]
    pivot_block = mm(basis, mm(diag_ref[...], basis, NN), TN)
    rotated = mm(row_basis[:, SKEL:], mm(merged_ref[...], basis, NN), TN)
    row = lax.broadcasted_iota(jnp.int32, (BLK, BLK), 0)
    eye = jnp.where(row == lax.broadcasted_iota(jnp.int32, (BLK, BLK), 1), 1.0, 0.0)
    inside = jnp.abs(lax.axis_index("row") // 2 - lax.axis_index("col")) <= (REACH + 1) // 2
    load_block(work, jnp.where(inside, pivot_block[:SKEL, :SKEL], eye))
    chol_inv(work)
    inverse = work[:, BLK:]
    folded = mm(inverse, mm(inverse, pivot_block[:SKEL, SKEL:], NN), TN)
    out_ref[...] = rotated[:, SKEL:] - mm(rotated[:, :SKEL], folded, NN)


def parent(merged, diag, row_basis, col_basis):
    return pl.pallas_call(
        parent_kernel,
        out_shape=jax.ShapeDtypeStruct((SKEL, SKEL), F32),
        in_specs=[pl.BlockSpec(memory_space=pltpu.VMEM)] * 4,
        out_specs=pl.BlockSpec(memory_space=pltpu.VMEM),
        scratch_shapes=[pltpu.VMEM((BLK, 2 * BLK), F32)],
        name="parent",
    )(merged, diag, row_basis, col_basis)


def from_behind(block, axis, distance):
    devices = range(lax.axis_size(axis))
    route = [(i - distance, i) for i in devices if i - distance in devices]
    return lax.ppermute(block, axis, route)


def local(near_blocks, leaf_bases, upper_bases, near_list):
    leaf_order = leaf_bases.shape[1]
    red_count = leaf_order - SKEL
    entry_count = near_blocks.shape[1]
    row_index = lax.axis_index("row")
    col_index = lax.axis_index("col")
    row_slot = row_index % 2
    holder = row_index // 2
    own_basis = leaf_bases[0]
    near_row = near_list[0]
    parent_reach = (REACH + 1) // 2
    upper_basis = upper_bases[0]
    pieces = []
    for offset in range(-parent_reach, parent_reach + 1):
        pieces.append(upper_basis if offset == 0 else from_behind(upper_basis, "col", -offset))
    basis_slot = jnp.clip(holder - col_index + parent_reach, 0, 2 * parent_reach)
    row_basis = lax.select_n(basis_slot, *pieces)

    def blank_pivot(near_tile, basis):
        return (
            jnp.zeros((red_count, red_count), F32),
            jnp.zeros((leaf_order, SKEL), F32),
        )

    factor, combined = lax.cond(
        col_index == 0, pivot, blank_pivot, near_blocks[0, 0], own_basis
    )
    mine = lax.dynamic_slice_in_dim(near_row, col_index * entry_count, entry_count, 0)
    slots = jnp.clip(mine - row_index + REACH, 0, 2 * REACH)
    leaves = jnp.arange(2 * lax.axis_size("col"), dtype=jnp.int32)
    matches = near_row[None, :] == leaves[:, None]
    first = jnp.argmax(matches, axis=1).astype(jnp.int32)
    places = col_index * entry_count + jnp.arange(entry_count, dtype=jnp.int32)
    picks = jnp.any(matches, axis=1)[:, None] & (first[:, None] == places[None, :])
    factor, merged, diag, strip = exchange(
        slots, picks.astype(jnp.int32).reshape(-1), near_blocks[0], own_basis[:, red_count:],
        combined, factor,
    )
    upper_full = parent(
        merged.reshape(2 * SKEL, 2 * SKEL), diag.reshape(2 * SKEL, 2 * SKEL), row_basis, upper_basis
    )
    upper_half = lax.dynamic_slice_in_dim(upper_full, row_slot * (SKEL // 2), SKEL // 2, 0)
    return (factor, strip, upper_half)


def solution(mesh):
    return jax.shard_map(
        local,
        mesh=mesh,
        in_specs=(
            P("row", "col", None, None),
            P("row", None, None),
            P("col", None, None),
            P("row", None),
        ),
        out_specs=(P("row", None), P("row", "col"), P("row", "col")),
        check_vma=False,
    )
```

```python
import functools

import jax
import jax.numpy as jnp
from jax import lax
from jax.experimental import pallas as pl
from jax.experimental.pallas import tpu as pltpu
from jax.sharding import PartitionSpec as P

SKEL = 128
REACH = 2
BLK = 128
PANEL = 8
CHUNKS = 4
F32 = jnp.float32
BF16 = jnp.bfloat16


def split(x):
    hi = x.astype(BF16)
    lo = (x - hi.astype(F32)).astype(BF16)
    return hi, lo


def mm(left, right, dims):
    lh, ll = split(left)
    rh, rl = split(right)
    dot = functools.partial(
        lax.dot_general, dimension_numbers=(dims, ((), ())), preferred_element_type=F32
    )
    return dot(lh, rh) + (dot(lh, rl) + dot(ll, rh))


NN = ((1,), (0,))
TN = ((0,), (0,))
NT = ((1,), (1,))


def panel_step(rows, base):
    width = rows.shape[1]
    sub = lax.broadcasted_iota(jnp.int32, (PANEL, 128), 0)
    cols = [
        jnp.broadcast_to(rows[:, base + t : base + t + 1], (PANEL, 128)) for t in range(PANEL)
    ]
    parts = [rows[:, c : c + 128] for c in range(0, width, 128)]
    for t in range(PANEL):
        scale = lax.rsqrt(cols[t][t : t + 1, :])
        mult = jnp.where(sub > t, cols[t] * scale, 0.0)
        for u in range(t + 1, PANEL):
            cols[u] = cols[u] - mult * (cols[u][t : t + 1, :] * scale)
        for c in range(len(parts)):
            lead = parts[c][t : t + 1, :] * scale
            parts[c] = jnp.where(sub == t, lead, parts[c] - mult * lead)
    return jnp.concatenate(parts, axis=1)


def chol_inv(work):
    for base in range(0, BLK, PANEL):
        rows = panel_step(work[base : base + PANEL, :], base)
        work[base : base + PANEL, :] = rows
        rest = BLK - base - PANEL
        if rest:
            high = rows.astype(BF16).astype(F32)
            low = rows - high
            left = jnp.concatenate([high, high, low, low], axis=0)[:, :BLK].astype(BF16)
            right = jnp.concatenate([high, low, high, low], axis=0).astype(BF16)
            update = lax.dot_general(
                left, right, (TN, ((), ())), preferred_element_type=F32
            )
            work[base + PANEL :, :] = work[base + PANEL :, :] - update[base + PANEL :, :]


def load_block(work, block):
    row = lax.broadcasted_iota(jnp.int32, (BLK, BLK), 0)
    col = lax.broadcasted_iota(jnp.int32, (BLK, BLK), 1)
    work[:, :BLK] = (block + block.T) * 0.5
    work[:, BLK:] = jnp.where(row == col, 1.0, 0.0)


def upper_part(block):
    row = lax.broadcasted_iota(jnp.int32, (BLK, BLK), 0)
    col = lax.broadcasted_iota(jnp.int32, (BLK, BLK), 1)
    return jnp.where(col >= row, block, 0.0)


def pivot_kernel(near_ref, basis_ref, factor_ref, combined_ref, mat, work):
    order = basis_ref.shape[0]
    red = order - SKEL
    count = red // BLK
    rotated = mm(basis_ref[:, :red], mm(near_ref[0], basis_ref[...], NN), TN)
    square = rotated[:, :red]
    mat[:, :red] = (square + square.T) * 0.5
    mat[:, red:] = rotated[:, red:]
    factor_ref[...] = jnp.zeros_like(factor_ref)
    inverses, leads = [], []
    for j in range(count):
        lo, hi = j * BLK, (j + 1) * BLK
        load_block(work, mat[lo:hi, lo:hi])
        chol_inv(work)
        factor_ref[lo:hi, lo:hi] = upper_part(work[:, :BLK]).T
        inverse = work[:, BLK:]
        lead = mm(inverse, mat[lo:hi, hi:], NN)
        if hi < red:
            factor_ref[hi:red, lo:hi] = lead[:, : red - hi].T
            mat[hi:red, hi:] = mat[hi:red, hi:] - mm(lead[:, : red - hi], lead, TN)
        inverses.append(inverse)
        leads.append(lead)
    folded = []
    for j in reversed(range(count)):
        rest = red - (j + 1) * BLK
        rhs = leads[j][:, rest:]
        if folded:
            rhs = rhs - mm(leads[j][:, :rest], jnp.concatenate(folded, axis=0), NN)
        folded.insert(0, mm(inverses[j], rhs, TN))
    combined_ref[...] = basis_ref[:, red:] - mm(
        basis_ref[:, :red], jnp.concatenate(folded, axis=0), NN
    )


def pivot(near, basis):
    order = basis.shape[0]
    red = order - SKEL
    return pl.pallas_call(
        pivot_kernel,
        out_shape=(
            jax.ShapeDtypeStruct((red, red), F32),
            jax.ShapeDtypeStruct((order, SKEL), F32),
        ),
        grid=(1,),
        in_specs=[
            pl.BlockSpec((1, order, order), lambda i: (0, 0, 0)),
            pl.BlockSpec((order, order), lambda i: (0, 0)),
        ],
        out_specs=[
            pl.BlockSpec((red, red), lambda i: (0, 0)),
            pl.BlockSpec((order, SKEL), lambda i: (0, 0)),
        ],
        scratch_shapes=[pltpu.VMEM((red, order), F32), pltpu.VMEM((BLK, 2 * BLK), F32)],
        compiler_params=pltpu.CompilerParams(vmem_limit_bytes=32 * 1024 * 1024),
        name="leaf_pivot",
    )(near, basis)


def exchange_kernel(
    rows, cols, list_ref, near_hbm, basis_ref, upper_ref, combined_ref, factor_in,
    factor_ref, merged_ref, diag_ref, strip_ref, row_basis_ref,
    near_ref, upper_half, table, products, outgoing, incoming,
    chain_send, chain_recv, row_send, row_recv, fact_send, fact_recv,
    tile_send, tile_recv, pair_send, pair_recv, diag_send, diag_recv,
    near_sem, basis_send, basis_recv,
):
    row = lax.axis_index("row")
    col = lax.axis_index("col")
    entries = near_hbm.shape[0]
    order = combined_ref.shape[0]
    red = order - SKEL
    step = order // CHUNKS
    reach_rows = 2 * ((REACH + 1) // 2) + 1
    holder = row // 2
    parity = row % 2
    parent_reach = (REACH + 1) // 2

    def remote(src, dst, send, recv, r, c):
        return pltpu.make_async_remote_copy(
            src_ref=src, dst_ref=dst, send_sem=send, recv_sem=recv,
            device_id=(r, c), device_id_type=pl.DeviceIdType.MESH,
        )

    loads = [
        pltpu.make_async_copy(near_hbm.at[e], near_ref.at[e], near_sem.at[e])
        for e in range(entries)
    ]
    for load in loads:
        load.start()

    def row_products():
        skel = basis_ref[:, red:]
        for e in range(entries):
            loads[e].wait()
            products[e] = mm(skel, near_ref[e], TN)

    upper_half[...] = upper_ref[:, SKEL:]
    row_basis_ref[...] = jnp.where(holder == col, upper_ref[:, SKEL:], 0.0)
    table[...] = jnp.zeros_like(table)
    diag_ref[...] = jnp.zeros_like(diag_ref)
    for lo in range(0, red - BLK, BLK):
        factor_ref[lo : lo + BLK, lo + BLK :] = jnp.zeros((BLK, red - lo - BLK), F32)

    barrier = pltpu.get_barrier_semaphore()
    for d in range(-reach_rows, reach_rows + 1):
        if d:
            pl.semaphore_signal(
                barrier, inc=1, device_id=(lax.rem(row + d + rows, rows), col),
                device_id_type=pl.DeviceIdType.MESH,
            )
    for d in range(1, cols):
        pl.semaphore_signal(
            barrier, inc=1, device_id=(row, lax.rem(col + d, cols)),
            device_id_type=pl.DeviceIdType.MESH,
        )

    @pl.when(col > 0)
    def _():
        row_products()

    pl.semaphore_wait(barrier, 2 * reach_rows + cols - 1)

    @pl.when(col == 0)
    def _():
        table[REACH] = combined_ref[...]

    def chunk(slot, k):
        return table.at[slot, pl.ds(k * step, step), :]

    def chain(k):
        return remote(
            chunk(REACH, k), chunk(REACH, k), chain_send.at[k], chain_recv.at[k], row,
            lax.rem(col + 1, cols),
        )

    def to_row(d, k):
        return remote(
            chunk(REACH, k), chunk(REACH - d, k), row_send.at[d + REACH, k],
            row_recv.at[REACH - d, k], lax.rem(row + d + rows, rows), col,
        )

    offsets = [d for d in range(-REACH, REACH + 1) if d]
    for k in range(CHUNKS):
        @pl.when(col > 0)
        def _():
            chain(k).wait_recv()

        @pl.when(col < cols - 1)
        def _():
            chain(k).start()

        for d in offsets:
            @pl.when((row + d >= 0) & (row + d < rows))
            def _():
                to_row(d, k).start()

    def strip(j):
        return factor_ref.at[pl.ds(j * BLK, BLK), pl.ds(0, (j + 1) * BLK)]

    def send_factor(j):
        return remote(
            strip(j), strip(j), fact_send.at[j], fact_recv.at[j], row, lax.rem(col + 1, cols)
        )

    def send_basis(d):
        return remote(
            upper_half, row_basis_ref, basis_send.at[d + parent_reach], basis_recv, row,
            lax.rem(col + d + cols, cols),
        )

    def sends_basis(d):
        return (holder == col) & (col + d >= 0) & (col + d < cols)

    @pl.when(col == 0)
    def _():
        factor_ref[...] = factor_in[...]
        for j in range(red // BLK):
            send_factor(j).start()
        row_products()

    for d in range(-parent_reach, parent_reach + 1):
        if d:
            @pl.when(sends_basis(d))
            def _():
                send_basis(d).start()

    def forward_factor():
        for j in range(red // BLK):
            send_factor(j).wait_recv()
            send_factor(j).start()

    @pl.when((col == 1) & (col < cols - 1))
    def _():
        forward_factor()

    for k in range(CHUNKS):
        for d in offsets:
            @pl.when((row + d >= 0) & (row + d < rows))
            def _():
                to_row(-d, k).wait_recv()

    own = [list_ref[0, col * entries + e] for e in range(entries)]
    leads = []
    for e in range(entries):
        seen = jnp.int32(0)
        for k in range(list_ref.shape[1]):
            same = (list_ref[0, k] == own[e]).astype(jnp.int32)
            before = (k < col * entries + e).astype(jnp.int32)
            seen = jnp.maximum(seen, same * before)
        leads.append(jnp.where(seen == 0, own[e], -1))
    tiles = []
    for e in range(entries):
        slot = jnp.clip(own[e] - row + REACH, 0, 2 * REACH)
        tiles.append(mm(products[e], table[slot], NN))
    zero = jnp.zeros((SKEL, SKEL), F32)
    for t in range(2 * cols):
        total = zero
        for e in range(entries):
            total = total + jnp.where(leads[e] == t, tiles[e], zero)
        outgoing[t // 2, :, (t % 2) * SKEL : (t % 2 + 1) * SKEL] = total

    def send_tile(d):
        other = lax.rem(col + d, cols)
        return remote(
            outgoing.at[other], incoming.at[d], tile_send.at[d], tile_recv.at[d], row, other
        )

    for d in range(1, cols):
        send_tile(d).start()

    @pl.when((col > 1) & (col < cols - 1))
    def _():
        forward_factor()

    total = outgoing[col]
    for d in range(1, cols):
        send_tile(d).wait_recv()
        total = total + incoming[d]
    strip_ref[...] = total
    merged_ref[parity] = total

    to_pair = remote(
        strip_ref, merged_ref.at[parity], pair_send, pair_recv, row + 1 - 2 * parity, col
    )
    to_pair.start()

    def to_diag(d):
        return remote(
            strip_ref, diag_ref.at[parity], diag_send.at[d + reach_rows],
            diag_recv.at[parity], lax.rem(row + d + rows, rows), col,
        )

    def sends_diag(d):
        other = row + d
        near = ((other + 2 * parent_reach) // 2 >= col) & (other // 2 <= col + parent_reach)
        return (holder == col) & (other >= 0) & (other < rows) & near

    @pl.when(holder == col)
    def _():
        diag_ref[parity] = total

    for d in range(-reach_rows, reach_rows + 1):
        if d:
            @pl.when(sends_diag(d))
            def _():
                to_diag(d).start()

    remote(
        strip_ref, merged_ref.at[1 - parity], pair_send, pair_recv, row + 1 - 2 * parity, col
    ).wait_recv()
    inside = (holder + parent_reach >= col) & (holder <= col + parent_reach)
    for s in range(2):
        @pl.when(inside & (row - 2 * col - s != 0))
        def _():
            remote(
                strip_ref, diag_ref.at[s], diag_send.at[0], diag_recv.at[s],
                row + 1 - 2 * parity, col,
            ).wait_recv()

    @pl.when((col == cols - 1) & (col > 0))
    def _():
        for j in range(red // BLK):
            send_factor(j).wait_recv()

    for d in range(-parent_reach, parent_reach + 1):
        if d:
            @pl.when(holder + d == col)
            def _():
                send_basis(d).wait_recv()

            @pl.when(sends_basis(d))
            def _():
                send_basis(d).wait_send()

    to_pair.wait_send()
    for d in range(-reach_rows, reach_rows + 1):
        if d:
            @pl.when(sends_diag(d))
            def _():
                to_diag(d).wait_send()
    for d in range(1, cols):
        send_tile(d).wait_send()
    for k in range(CHUNKS):
        @pl.when(col < cols - 1)
        def _():
            chain(k).wait_send()

        for d in offsets:
            @pl.when((row + d >= 0) & (row + d < rows))
            def _():
                to_row(d, k).wait_send()

    @pl.when(col < cols - 1)
    def _():
        for j in range(red // BLK):
            send_factor(j).wait_send()


def exchange(near_row, near, basis, upper_basis, combined, factor):
    rows, cols = lax.axis_size("row"), lax.axis_size("col")
    order = combined.shape[0]
    red = factor.shape[0]
    entries = near.shape[0]
    reach_rows = 2 * ((REACH + 1) // 2) + 1
    spans = 2 * REACH + 1
    vmem = pl.BlockSpec(memory_space=pltpu.VMEM)
    smem = pl.BlockSpec(memory_space=pltpu.SMEM)
    dma = pltpu.SemaphoreType.DMA
    return pl.pallas_call(
        functools.partial(exchange_kernel, rows, cols),
        out_shape=(
            jax.ShapeDtypeStruct((red, red), F32),
            jax.ShapeDtypeStruct((2, SKEL, 2 * SKEL), F32),
            jax.ShapeDtypeStruct((2, SKEL, 2 * SKEL), F32),
            jax.ShapeDtypeStruct((SKEL, 2 * SKEL), F32),
            jax.ShapeDtypeStruct((2 * SKEL, SKEL), F32),
        ),
        in_specs=[smem, pl.BlockSpec(memory_space=pl.ANY), vmem, vmem, vmem, vmem],
        out_specs=[vmem] * 5,
        scratch_shapes=[
            pltpu.VMEM(near.shape, F32),
            pltpu.VMEM((2 * SKEL, SKEL), F32),
            pltpu.VMEM((spans, order, SKEL), F32),
            pltpu.VMEM((entries, SKEL, order), F32),
            pltpu.VMEM((cols, SKEL, 2 * SKEL), F32),
            pltpu.VMEM((cols, SKEL, 2 * SKEL), F32),
            dma((CHUNKS,)), dma((CHUNKS,)),
            dma((spans, CHUNKS)), dma((spans, CHUNKS)),
            dma((red // BLK,)), dma((red // BLK,)),
            dma((cols,)), dma((cols,)),
            dma, dma,
            dma((2 * reach_rows + 1,)), dma((2,)),
            dma((entries,)), dma((2 * ((REACH + 1) // 2) + 1,)), dma,
        ],
        compiler_params=pltpu.CompilerParams(
            collective_id=0, has_side_effects=True, vmem_limit_bytes=40 * 1024 * 1024
        ),
        name="exchange",
    )(near_row, near, basis, upper_basis, combined, factor)


def parent_kernel(merged_ref, diag_ref, row_basis, col_basis, out_ref, work):
    basis = col_basis[...]
    pivot_block = mm(basis, mm(diag_ref[...], basis, NN), TN)
    rotated = mm(row_basis[...], mm(merged_ref[...], basis, NN), TN)
    row = lax.broadcasted_iota(jnp.int32, (BLK, BLK), 0)
    eye = jnp.where(row == lax.broadcasted_iota(jnp.int32, (BLK, BLK), 1), 1.0, 0.0)
    inside = jnp.abs(lax.axis_index("row") // 2 - lax.axis_index("col")) <= (REACH + 1) // 2
    load_block(work, jnp.where(inside, pivot_block[:SKEL, :SKEL], eye))
    chol_inv(work)
    inverse = work[:, BLK:]
    folded = mm(inverse, mm(inverse, pivot_block[:SKEL, SKEL:], NN), TN)
    full = rotated[:, SKEL:] - mm(rotated[:, :SKEL], folded, NN)
    half = SKEL // 2
    out_ref[...] = jnp.where(lax.axis_index("row") % 2 == 0, full[:half], full[half:])


def parent(merged, diag, row_basis, col_basis):
    return pl.pallas_call(
        parent_kernel,
        out_shape=jax.ShapeDtypeStruct((SKEL // 2, SKEL), F32),
        in_specs=[pl.BlockSpec(memory_space=pltpu.VMEM)] * 4,
        out_specs=pl.BlockSpec(memory_space=pltpu.VMEM),
        scratch_shapes=[pltpu.VMEM((BLK, 2 * BLK), F32)],
        name="parent",
    )(merged, diag, row_basis, col_basis)


def local(near_blocks, leaf_bases, upper_bases, near_list):
    order = leaf_bases.shape[1]
    red = order - SKEL
    near, basis, upper_basis = near_blocks[0], leaf_bases[0], upper_bases[0]

    def blank_pivot(near, basis):
        return jnp.zeros((red, red), F32), jnp.zeros((order, SKEL), F32)

    factor, combined = lax.cond(lax.axis_index("col") == 0, pivot, blank_pivot, near, basis)
    factor, merged, diag, strip, row_basis = exchange(
        near_list, near, basis, upper_basis, combined, factor
    )
    upper_half = parent(
        merged.reshape(2 * SKEL, 2 * SKEL), diag.reshape(2 * SKEL, 2 * SKEL), row_basis, upper_basis
    )
    return (factor, strip, upper_half)


def solution(mesh):
    return jax.shard_map(
        local,
        mesh=mesh,
        in_specs=(
            P("row", "col", None, None),
            P("row", None, None),
            P("col", None, None),
            P("row", None),
        ),
        out_specs=(P("row", None), P("row", "col"), P("row", "col")),
        check_vma=False,
    )
```

```python
import functools

import jax
import jax.numpy as jnp
from jax import lax
from jax.experimental import pallas as pl
from jax.experimental.pallas import tpu as pltpu
from jax.sharding import PartitionSpec as P

SKEL = 128
REACH = 2
BLK = 128
PANEL = 8
CHUNKS = 4
F32 = jnp.float32
BF16 = jnp.bfloat16


def split(x):
    hi = x.astype(BF16)
    lo = (x - hi.astype(F32)).astype(BF16)
    return hi, lo


def mm(left, right, dims):
    lh, ll = split(left)
    rh, rl = split(right)
    dot = functools.partial(
        lax.dot_general, dimension_numbers=(dims, ((), ())), preferred_element_type=F32
    )
    return dot(lh, rh) + (dot(lh, rl) + dot(ll, rh))


NN = ((1,), (0,))
TN = ((0,), (0,))
NT = ((1,), (1,))


def panel_step(rows, base):
    width = rows.shape[1]
    sub = lax.broadcasted_iota(jnp.int32, (PANEL, 128), 0)
    cols = [
        jnp.broadcast_to(rows[:, base + t : base + t + 1], (PANEL, 128)) for t in range(PANEL)
    ]
    parts = [rows[:, c : c + 128] for c in range(0, width, 128)]
    for t in range(PANEL):
        scale = lax.rsqrt(cols[t][t : t + 1, :])
        mult = jnp.where(sub > t, cols[t] * scale, 0.0)
        for u in range(t + 1, PANEL):
            cols[u] = cols[u] - mult * (cols[u][t : t + 1, :] * scale)
        for c in range(len(parts)):
            lead = parts[c][t : t + 1, :] * scale
            parts[c] = jnp.where(sub == t, lead, parts[c] - mult * lead)
    return jnp.concatenate(parts, axis=1)


def chol_inv(work):
    for base in range(0, BLK, PANEL):
        rows = panel_step(work[base : base + PANEL, :], base)
        work[base : base + PANEL, :] = rows
        rest = BLK - base - PANEL
        if rest:
            high = rows.astype(BF16).astype(F32)
            low = rows - high
            left = jnp.concatenate([high, high, low, low], axis=0)[:, :BLK].astype(BF16)
            right = jnp.concatenate([high, low, high, low], axis=0).astype(BF16)
            update = lax.dot_general(
                left, right, (TN, ((), ())), preferred_element_type=F32
            )
            work[base + PANEL :, :] = work[base + PANEL :, :] - update[base + PANEL :, :]


def load_block(work, block):
    row = lax.broadcasted_iota(jnp.int32, (BLK, BLK), 0)
    col = lax.broadcasted_iota(jnp.int32, (BLK, BLK), 1)
    work[:, :BLK] = (block + block.T) * 0.5
    work[:, BLK:] = jnp.where(row == col, 1.0, 0.0)


def upper_part(block):
    row = lax.broadcasted_iota(jnp.int32, (BLK, BLK), 0)
    col = lax.broadcasted_iota(jnp.int32, (BLK, BLK), 1)
    return jnp.where(col >= row, block, 0.0)


def pivot_kernel(near_ref, basis_ref, factor_ref, combined_ref, mat, work):
    order = basis_ref.shape[0]
    red = order - SKEL
    count = red // BLK
    rotated = mm(basis_ref[:, :red], mm(near_ref[0], basis_ref[...], NN), TN)
    square = rotated[:, :red]
    mat[:, :red] = (square + square.T) * 0.5
    mat[:, red:] = rotated[:, red:]
    factor_ref[...] = jnp.zeros_like(factor_ref)
    inverses, leads = [], []
    for j in range(count):
        lo, hi = j * BLK, (j + 1) * BLK
        load_block(work, mat[lo:hi, lo:hi])
        chol_inv(work)
        factor_ref[lo:hi, lo:hi] = upper_part(work[:, :BLK]).T
        inverse = work[:, BLK:]
        lead = mm(inverse, mat[lo:hi, hi:], NN)
        if hi < red:
            factor_ref[hi:red, lo:hi] = lead[:, : red - hi].T
            mat[hi:red, hi:] = mat[hi:red, hi:] - mm(lead[:, : red - hi], lead, TN)
        inverses.append(inverse)
        leads.append(lead)
    folded = []
    for j in reversed(range(count)):
        rest = red - (j + 1) * BLK
        rhs = leads[j][:, rest:]
        if folded:
            rhs = rhs - mm(leads[j][:, :rest], jnp.concatenate(folded, axis=0), NN)
        folded.insert(0, mm(inverses[j], rhs, TN))
    combined_ref[...] = basis_ref[:, red:] - mm(
        basis_ref[:, :red], jnp.concatenate(folded, axis=0), NN
    )


def pivot(near, basis):
    order = basis.shape[0]
    red = order - SKEL
    return pl.pallas_call(
        pivot_kernel,
        out_shape=(
            jax.ShapeDtypeStruct((red, red), F32),
            jax.ShapeDtypeStruct((order, SKEL), F32),
        ),
        grid=(1,),
        in_specs=[
            pl.BlockSpec((1, order, order), lambda i: (0, 0, 0)),
            pl.BlockSpec((order, order), lambda i: (0, 0)),
        ],
        out_specs=[
            pl.BlockSpec((red, red), lambda i: (0, 0)),
            pl.BlockSpec((order, SKEL), lambda i: (0, 0)),
        ],
        scratch_shapes=[pltpu.VMEM((red, order), F32), pltpu.VMEM((BLK, 2 * BLK), F32)],
        compiler_params=pltpu.CompilerParams(vmem_limit_bytes=32 * 1024 * 1024),
        name="leaf_pivot",
    )(near, basis)


def exchange_kernel(
    rows, cols, list_ref, near_hbm, basis_ref, upper_ref, combined_ref, factor_in,
    factor_ref, merged_ref, diag_ref, strip_ref, row_basis_ref,
    near_ref, upper_half, table, products, outgoing, incoming,
    chain_send, chain_recv, row_send, row_recv, fact_send, fact_recv,
    tile_send, tile_recv, pair_send, pair_recv, diag_send, diag_recv,
    near_sem, basis_send, basis_recv,
):
    row = lax.axis_index("row")
    col = lax.axis_index("col")
    entries = near_hbm.shape[0]
    order = combined_ref.shape[0]
    red = order - SKEL
    step = order // CHUNKS
    reach_rows = 2 * ((REACH + 1) // 2) + 1
    holder = row // 2
    parity = row % 2
    parent_reach = (REACH + 1) // 2

    def remote(src, dst, send, recv, r, c):
        return pltpu.make_async_remote_copy(
            src_ref=src, dst_ref=dst, send_sem=send, recv_sem=recv,
            device_id=(r, c), device_id_type=pl.DeviceIdType.MESH,
        )

    loads = [
        pltpu.make_async_copy(near_hbm.at[e], near_ref.at[e], near_sem.at[e])
        for e in range(entries)
    ]
    for load in loads:
        load.start()

    def row_products():
        skel = basis_ref[:, red:]
        for e in range(entries):
            loads[e].wait()
            products[e] = mm(skel, near_ref[e], TN)

    upper_half[...] = upper_ref[:, SKEL:]
    row_basis_ref[...] = jnp.where(holder == col, upper_ref[:, SKEL:], 0.0)
    table[...] = jnp.zeros_like(table)
    diag_ref[...] = jnp.zeros_like(diag_ref)
    for lo in range(0, red - BLK, BLK):
        factor_ref[lo : lo + BLK, lo + BLK :] = jnp.zeros((BLK, red - lo - BLK), F32)

    barrier = pltpu.get_barrier_semaphore()
    for d in range(-reach_rows, reach_rows + 1):
        if d:
            pl.semaphore_signal(
                barrier, inc=1, device_id=(lax.rem(row + d + rows, rows), col),
                device_id_type=pl.DeviceIdType.MESH,
            )
    for d in range(1, cols):
        pl.semaphore_signal(
            barrier, inc=1, device_id=(row, lax.rem(col + d, cols)),
            device_id_type=pl.DeviceIdType.MESH,
        )

    @pl.when(col > 0)
    def _():
        row_products()

    pl.semaphore_wait(barrier, 2 * reach_rows + cols - 1)

    @pl.when(col == 0)
    def _():
        table[REACH] = combined_ref[...]

    def chunk(slot, k):
        return table.at[slot, pl.ds(k * step, step), :]

    def chain(k):
        return remote(
            chunk(REACH, k), chunk(REACH, k), chain_send.at[k], chain_recv.at[k], row,
            lax.rem(col + 1, cols),
        )

    def to_row(d, k):
        return remote(
            chunk(REACH, k), chunk(REACH - d, k), row_send.at[d + REACH, k],
            row_recv.at[REACH - d, k], lax.rem(row + d + rows, rows), col,
        )

    offsets = [d for d in range(-REACH, REACH + 1) if d]
    toward = 1 - 2 * parity

    def valid(d):
        return (row + d >= 0) & (row + d < rows)

    def direct(d):
        return valid(d) & ((d % 2 == 0) | (toward == d))

    def relay(k):
        return remote(
            chunk(REACH + 2 * toward, k), chunk(REACH + toward, k),
            row_send.at[REACH - toward, k], row_recv.at[REACH + toward, k],
            row + toward, col,
        )

    def relays():
        return (row + 2 * toward >= 0) & (row + 2 * toward < rows)

    for k in range(CHUNKS):
        @pl.when(col > 0)
        def _():
            chain(k).wait_recv()

        @pl.when(col < cols - 1)
        def _():
            chain(k).start()

        for d in offsets:
            @pl.when(direct(d))
            def _():
                to_row(d, k).start()

    def strip(j):
        return factor_ref.at[pl.ds(j * BLK, BLK), pl.ds(0, (j + 1) * BLK)]

    def send_factor(j):
        return remote(
            strip(j), strip(j), fact_send.at[j], fact_recv.at[j], row, lax.rem(col + 1, cols)
        )

    def send_basis(d):
        return remote(
            upper_half, row_basis_ref, basis_send.at[d + parent_reach], basis_recv, row,
            lax.rem(col + d + cols, cols),
        )

    def sends_basis(d):
        return (holder == col) & (col + d >= 0) & (col + d < cols)

    @pl.when(col == 0)
    def _():
        factor_ref[...] = factor_in[...]
        for j in range(red // BLK):
            send_factor(j).start()
        row_products()

    for d in range(-parent_reach, parent_reach + 1):
        if d:
            @pl.when(sends_basis(d))
            def _():
                send_basis(d).start()

    def forward_factor():
        for j in range(red // BLK):
            send_factor(j).wait_recv()
            send_factor(j).start()

    @pl.when((col == 1) & (col < cols - 1))
    def _():
        forward_factor()

    for k in range(CHUNKS):
        @pl.when(relays())
        def _():
            remote(
                chunk(REACH, k), chunk(REACH + 2 * toward, k), row_send.at[0, k],
                row_recv.at[REACH + 2 * toward, k], row + toward, col,
            ).wait_recv()
            relay(k).start()

    for k in range(CHUNKS):
        for d in offsets:
            waiting = valid(d) if d % 2 else valid(d) & (2 * toward != d)

            @pl.when(waiting)
            def _():
                to_row(-d, k).wait_recv()

    own = [list_ref[0, col * entries + e] for e in range(entries)]
    leads = []
    for e in range(entries):
        seen = jnp.int32(0)
        for k in range(list_ref.shape[1]):
            same = (list_ref[0, k] == own[e]).astype(jnp.int32)
            before = (k < col * entries + e).astype(jnp.int32)
            seen = jnp.maximum(seen, same * before)
        leads.append(jnp.where(seen == 0, own[e], -1))
    tiles = []
    for e in range(entries):
        slot = jnp.clip(own[e] - row + REACH, 0, 2 * REACH)
        tiles.append(mm(products[e], table[slot], NN))
    zero = jnp.zeros((SKEL, SKEL), F32)
    for t in range(2 * cols):
        total = zero
        for e in range(entries):
            total = total + jnp.where(leads[e] == t, tiles[e], zero)
        outgoing[t // 2, :, (t % 2) * SKEL : (t % 2 + 1) * SKEL] = total

    def send_tile(d):
        other = lax.rem(col + d, cols)
        return remote(
            outgoing.at[other], incoming.at[d], tile_send.at[d], tile_recv.at[d], row, other
        )

    for d in range(1, cols):
        send_tile(d).start()

    @pl.when((col > 1) & (col < cols - 1))
    def _():
        forward_factor()

    total = outgoing[col]
    for d in range(1, cols):
        send_tile(d).wait_recv()
        total = total + incoming[d]
    strip_ref[...] = total
    merged_ref[parity] = total

    to_pair = remote(
        strip_ref, merged_ref.at[parity], pair_send, pair_recv, row + 1 - 2 * parity, col
    )
    to_pair.start()

    def to_diag(d):
        return remote(
            strip_ref, diag_ref.at[parity], diag_send.at[d + reach_rows],
            diag_recv.at[parity], lax.rem(row + d + rows, rows), col,
        )

    def sends_diag(d):
        other = row + d
        near = ((other + 2 * parent_reach) // 2 >= col) & (other // 2 <= col + parent_reach)
        return (holder == col) & valid(d) & near & ((d % 2 == 0) | (toward == d))

    @pl.when(holder == col)
    def _():
        diag_ref[parity] = total

    for d in (-2, -1, 1, 2):
        @pl.when(sends_diag(d))
        def _():
            to_diag(d).start()

    remote(
        strip_ref, merged_ref.at[1 - parity], pair_send, pair_recv, row + 1 - 2 * parity, col
    ).wait_recv()
    inside = (holder + parent_reach >= col) & (holder <= col + parent_reach)

    def from_diag(s):
        return remote(
            diag_ref.at[s], diag_ref.at[s], diag_send.at[0], diag_recv.at[s], row + toward, col
        )

    @pl.when(inside & (holder != col))
    def _():
        from_diag(parity).wait_recv()
        from_diag(parity).start()

    @pl.when(inside)
    def _():
        from_diag(1 - parity).wait_recv()

    @pl.when((col == cols - 1) & (col > 0))
    def _():
        for j in range(red // BLK):
            send_factor(j).wait_recv()

    for d in range(-parent_reach, parent_reach + 1):
        if d:
            @pl.when(holder + d == col)
            def _():
                send_basis(d).wait_recv()

            @pl.when(sends_basis(d))
            def _():
                send_basis(d).wait_send()

    @pl.when(inside & (holder != col))
    def _():
        from_diag(parity).wait_send()

    to_pair.wait_send()
    for d in (-2, -1, 1, 2):
        @pl.when(sends_diag(d))
        def _():
            to_diag(d).wait_send()
    for d in range(1, cols):
        send_tile(d).wait_send()
    for k in range(CHUNKS):
        @pl.when(col < cols - 1)
        def _():
            chain(k).wait_send()

        for d in offsets:
            @pl.when(direct(d))
            def _():
                to_row(d, k).wait_send()

        @pl.when(relays())
        def _():
            relay(k).wait_send()

    @pl.when(col < cols - 1)
    def _():
        for j in range(red // BLK):
            send_factor(j).wait_send()


def exchange(near_row, near, basis, upper_basis, combined, factor):
    rows, cols = lax.axis_size("row"), lax.axis_size("col")
    order = combined.shape[0]
    red = factor.shape[0]
    entries = near.shape[0]
    reach_rows = 2 * ((REACH + 1) // 2) + 1
    spans = 2 * REACH + 1
    vmem = pl.BlockSpec(memory_space=pltpu.VMEM)
    smem = pl.BlockSpec(memory_space=pltpu.SMEM)
    dma = pltpu.SemaphoreType.DMA
    return pl.pallas_call(
        functools.partial(exchange_kernel, rows, cols),
        out_shape=(
            jax.ShapeDtypeStruct((red, red), F32),
            jax.ShapeDtypeStruct((2, SKEL, 2 * SKEL), F32),
            jax.ShapeDtypeStruct((2, SKEL, 2 * SKEL), F32),
            jax.ShapeDtypeStruct((SKEL, 2 * SKEL), F32),
            jax.ShapeDtypeStruct((2 * SKEL, SKEL), F32),
        ),
        in_specs=[smem, pl.BlockSpec(memory_space=pl.ANY), vmem, vmem, vmem, vmem],
        out_specs=[vmem] * 5,
        scratch_shapes=[
            pltpu.VMEM(near.shape, F32),
            pltpu.VMEM((2 * SKEL, SKEL), F32),
            pltpu.VMEM((spans, order, SKEL), F32),
            pltpu.VMEM((entries, SKEL, order), F32),
            pltpu.VMEM((cols, SKEL, 2 * SKEL), F32),
            pltpu.VMEM((cols, SKEL, 2 * SKEL), F32),
            dma((CHUNKS,)), dma((CHUNKS,)),
            dma((spans, CHUNKS)), dma((spans, CHUNKS)),
            dma((red // BLK,)), dma((red // BLK,)),
            dma((cols,)), dma((cols,)),
            dma, dma,
            dma((2 * reach_rows + 1,)), dma((2,)),
            dma((entries,)), dma((2 * ((REACH + 1) // 2) + 1,)), dma,
        ],
        compiler_params=pltpu.CompilerParams(
            collective_id=0, has_side_effects=True, vmem_limit_bytes=40 * 1024 * 1024
        ),
        name="exchange",
    )(near_row, near, basis, upper_basis, combined, factor)


def parent_kernel(merged_ref, diag_ref, row_basis, col_basis, out_ref, work):
    basis = col_basis[...]
    pivot_block = mm(basis, mm(diag_ref[...], basis, NN), TN)
    rotated = mm(row_basis[...], mm(merged_ref[...], basis, NN), TN)
    row = lax.broadcasted_iota(jnp.int32, (BLK, BLK), 0)
    eye = jnp.where(row == lax.broadcasted_iota(jnp.int32, (BLK, BLK), 1), 1.0, 0.0)
    inside = jnp.abs(lax.axis_index("row") // 2 - lax.axis_index("col")) <= (REACH + 1) // 2
    load_block(work, jnp.where(inside, pivot_block[:SKEL, :SKEL], eye))
    chol_inv(work)
    inverse = work[:, BLK:]
    folded = mm(inverse, mm(inverse, pivot_block[:SKEL, SKEL:], NN), TN)
    full = rotated[:, SKEL:] - mm(rotated[:, :SKEL], folded, NN)
    half = SKEL // 2
    out_ref[...] = jnp.where(lax.axis_index("row") % 2 == 0, full[:half], full[half:])


def parent(merged, diag, row_basis, col_basis):
    return pl.pallas_call(
        parent_kernel,
        out_shape=jax.ShapeDtypeStruct((SKEL // 2, SKEL), F32),
        in_specs=[pl.BlockSpec(memory_space=pltpu.VMEM)] * 4,
        out_specs=pl.BlockSpec(memory_space=pltpu.VMEM),
        scratch_shapes=[pltpu.VMEM((BLK, 2 * BLK), F32)],
        name="parent",
    )(merged, diag, row_basis, col_basis)


def local(near_blocks, leaf_bases, upper_bases, near_list):
    order = leaf_bases.shape[1]
    red = order - SKEL
    near, basis, upper_basis = near_blocks[0], leaf_bases[0], upper_bases[0]

    def blank_pivot(near, basis):
        return jnp.zeros((red, red), F32), jnp.zeros((order, SKEL), F32)

    factor, combined = lax.cond(lax.axis_index("col") == 0, pivot, blank_pivot, near, basis)
    factor, merged, diag, strip, row_basis = exchange(
        near_list, near, basis, upper_basis, combined, factor
    )
    upper_half = parent(
        merged.reshape(2 * SKEL, 2 * SKEL), diag.reshape(2 * SKEL, 2 * SKEL), row_basis, upper_basis
    )
    return (factor, strip, upper_half)


def solution(mesh):
    return jax.shard_map(
        local,
        mesh=mesh,
        in_specs=(
            P("row", "col", None, None),
            P("row", None, None),
            P("col", None, None),
            P("row", None),
        ),
        out_specs=(P("row", None), P("row", "col"), P("row", "col")),
        check_vma=False,
    )
```

```python
import functools

import jax
import jax.numpy as jnp
from jax import lax
from jax.experimental import pallas as pl
from jax.experimental.pallas import tpu as pltpu
from jax.sharding import PartitionSpec as P

SKEL = 128
REACH = 2
BLK = 128
PANEL = 8
CHUNKS = 4
F32 = jnp.float32
BF16 = jnp.bfloat16


def split(x):
    hi = x.astype(BF16)
    lo = (x - hi.astype(F32)).astype(BF16)
    return hi, lo


def mm(left, right, dims):
    lh, ll = split(left)
    rh, rl = split(right)
    dot = functools.partial(
        lax.dot_general, dimension_numbers=(dims, ((), ())), preferred_element_type=F32
    )
    return dot(lh, rh) + (dot(lh, rl) + dot(ll, rh))


NN = ((1,), (0,))
TN = ((0,), (0,))
NT = ((1,), (1,))


def panel_step(rows, base):
    width = rows.shape[1]
    sub = lax.broadcasted_iota(jnp.int32, (PANEL, 128), 0)
    cols = [
        jnp.broadcast_to(rows[:, base + t : base + t + 1], (PANEL, 128)) for t in range(PANEL)
    ]
    parts = [rows[:, c : c + 128] for c in range(0, width, 128)]
    for t in range(PANEL):
        scale = lax.rsqrt(cols[t][t : t + 1, :])
        mult = jnp.where(sub > t, cols[t] * scale, 0.0)
        for u in range(t + 1, PANEL):
            cols[u] = cols[u] - mult * (cols[u][t : t + 1, :] * scale)
        for c in range(len(parts)):
            lead = parts[c][t : t + 1, :] * scale
            parts[c] = jnp.where(sub == t, lead, parts[c] - mult * lead)
    return jnp.concatenate(parts, axis=1)


def chol_inv(work):
    for base in range(0, BLK, PANEL):
        rows = panel_step(work[base : base + PANEL, :], base)
        work[base : base + PANEL, :] = rows
        rest = BLK - base - PANEL
        if rest:
            high = rows.astype(BF16).astype(F32)
            low = rows - high
            left = jnp.concatenate([high, high, low, low], axis=0)[:, :BLK].astype(BF16)
            right = jnp.concatenate([high, low, high, low], axis=0).astype(BF16)
            update = lax.dot_general(
                left, right, (TN, ((), ())), preferred_element_type=F32
            )
            work[base + PANEL :, :] = work[base + PANEL :, :] - update[base + PANEL :, :]


def load_block(work, block):
    row = lax.broadcasted_iota(jnp.int32, (BLK, BLK), 0)
    col = lax.broadcasted_iota(jnp.int32, (BLK, BLK), 1)
    work[:, :BLK] = (block + block.T) * 0.5
    work[:, BLK:] = jnp.where(row == col, 1.0, 0.0)


def upper_part(block):
    row = lax.broadcasted_iota(jnp.int32, (BLK, BLK), 0)
    col = lax.broadcasted_iota(jnp.int32, (BLK, BLK), 1)
    return jnp.where(col >= row, block, 0.0)


def pivot_kernel(near_ref, basis_ref, factor_ref, combined_ref, mat, work):
    order = basis_ref.shape[0]
    red = order - SKEL
    count = red // BLK
    rotated = mm(basis_ref[:, :red], mm(near_ref[0], basis_ref[...], NN), TN)
    square = rotated[:, :red]
    mat[:, :red] = (square + square.T) * 0.5
    mat[:, red:] = rotated[:, red:]
    factor_ref[...] = jnp.zeros_like(factor_ref)
    inverses, leads = [], []
    for j in range(count):
        lo, hi = j * BLK, (j + 1) * BLK
        load_block(work, mat[lo:hi, lo:hi])
        chol_inv(work)
        factor_ref[lo:hi, lo:hi] = upper_part(work[:, :BLK]).T
        inverse = work[:, BLK:]
        lead = mm(inverse, mat[lo:hi, hi:], NN)
        if hi < red:
            factor_ref[hi:red, lo:hi] = lead[:, : red - hi].T
            mat[hi:red, hi:] = mat[hi:red, hi:] - mm(lead[:, : red - hi], lead, TN)
        inverses.append(inverse)
        leads.append(lead)
    folded = []
    for j in reversed(range(count)):
        rest = red - (j + 1) * BLK
        rhs = leads[j][:, rest:]
        if folded:
            rhs = rhs - mm(leads[j][:, :rest], jnp.concatenate(folded, axis=0), NN)
        folded.insert(0, mm(inverses[j], rhs, TN))
    combined_ref[...] = basis_ref[:, red:] - mm(
        basis_ref[:, :red], jnp.concatenate(folded, axis=0), NN
    )


def pivot(near, basis):
    order = basis.shape[0]
    red = order - SKEL
    return pl.pallas_call(
        pivot_kernel,
        out_shape=(
            jax.ShapeDtypeStruct((red, red), F32),
            jax.ShapeDtypeStruct((order, SKEL), F32),
        ),
        grid=(1,),
        in_specs=[
            pl.BlockSpec((1, order, order), lambda i: (0, 0, 0)),
            pl.BlockSpec((order, order), lambda i: (0, 0)),
        ],
        out_specs=[
            pl.BlockSpec((red, red), lambda i: (0, 0)),
            pl.BlockSpec((order, SKEL), lambda i: (0, 0)),
        ],
        scratch_shapes=[pltpu.VMEM((red, order), F32), pltpu.VMEM((BLK, 2 * BLK), F32)],
        compiler_params=pltpu.CompilerParams(vmem_limit_bytes=32 * 1024 * 1024),
        name="leaf_pivot",
    )(near, basis)


def exchange_kernel(
    rows, cols, list_ref, near_hbm, basis_ref, upper_ref, combined_ref, factor_in,
    factor_ref, merged_ref, diag_ref, strip_ref, row_basis_ref,
    near_ref, upper_half, table, products, outgoing, incoming,
    chain_send, chain_recv, row_send, row_recv, fact_send, fact_recv,
    tile_send, tile_recv, pair_send, pair_recv, diag_send, diag_recv,
    near_sem, basis_send, basis_recv,
):
    row = lax.axis_index("row")
    col = lax.axis_index("col")
    entries = near_hbm.shape[0]
    order = combined_ref.shape[0]
    red = order - SKEL
    step = order // CHUNKS
    reach_rows = 2 * ((REACH + 1) // 2) + 1
    holder = row // 2
    parity = row % 2
    parent_reach = (REACH + 1) // 2

    def remote(src, dst, send, recv, r, c):
        return pltpu.make_async_remote_copy(
            src_ref=src, dst_ref=dst, send_sem=send, recv_sem=recv,
            device_id=(r, c), device_id_type=pl.DeviceIdType.MESH,
        )

    loads = [
        pltpu.make_async_copy(near_hbm.at[e], near_ref.at[e], near_sem.at[e])
        for e in range(entries)
    ]
    for load in loads:
        load.start()

    def row_products():
        skel = basis_ref[:, red:]
        for e in range(entries):
            loads[e].wait()
            products[e] = mm(skel, near_ref[e], TN)

    upper_half[...] = upper_ref[:, SKEL:]
    row_basis_ref[...] = jnp.where(holder == col, upper_ref[:, SKEL:], 0.0)
    table[...] = jnp.zeros_like(table)
    incoming[...] = jnp.zeros_like(incoming)
    diag_ref[...] = jnp.zeros_like(diag_ref)
    for lo in range(0, red - BLK, BLK):
        factor_ref[lo : lo + BLK, lo + BLK :] = jnp.zeros((BLK, red - lo - BLK), F32)

    barrier = pltpu.get_barrier_semaphore()
    for d in range(-reach_rows, reach_rows + 1):
        if d:
            pl.semaphore_signal(
                barrier, inc=1, device_id=(lax.rem(row + d + rows, rows), col),
                device_id_type=pl.DeviceIdType.MESH,
            )
    for d in range(1, cols):
        pl.semaphore_signal(
            barrier, inc=1, device_id=(row, lax.rem(col + d, cols)),
            device_id_type=pl.DeviceIdType.MESH,
        )

    @pl.when(col > 0)
    def _():
        row_products()

    pl.semaphore_wait(barrier, 2 * reach_rows + cols - 1)

    @pl.when(col == 0)
    def _():
        table[REACH] = combined_ref[...]

    def chunk(slot, k):
        return table.at[slot, pl.ds(k * step, step), :]

    def chain(k):
        return remote(
            chunk(REACH, k), chunk(REACH, k), chain_send.at[k], chain_recv.at[k], row,
            lax.rem(col + 1, cols),
        )

    def to_row(d, k):
        return remote(
            chunk(REACH, k), chunk(REACH - d, k), row_send.at[d + REACH, k],
            row_recv.at[REACH - d, k], lax.rem(row + d + rows, rows), col,
        )

    offsets = [d for d in range(-REACH, REACH + 1) if d]
    toward = 1 - 2 * parity

    def valid(d):
        return (row + d >= 0) & (row + d < rows)

    def direct(d):
        return valid(d) & ((d % 2 == 0) | (toward == d))

    def relay(k):
        return remote(
            chunk(REACH + 2 * toward, k), chunk(REACH + toward, k),
            row_send.at[REACH - toward, k], row_recv.at[REACH + toward, k],
            row + toward, col,
        )

    def relays():
        return (row + 2 * toward >= 0) & (row + 2 * toward < rows)

    for k in range(CHUNKS):
        @pl.when(col > 0)
        def _():
            chain(k).wait_recv()

        @pl.when(col < cols - 1)
        def _():
            chain(k).start()

        for d in offsets:
            @pl.when(direct(d))
            def _():
                to_row(d, k).start()

    def strip(j):
        return factor_ref.at[pl.ds(j * BLK, BLK), pl.ds(0, (j + 1) * BLK)]

    def send_factor(j):
        return remote(
            strip(j), strip(j), fact_send.at[j], fact_recv.at[j], row, lax.rem(col + 1, cols)
        )

    def send_basis(d):
        return remote(
            upper_half, row_basis_ref, basis_send.at[d + parent_reach], basis_recv, row,
            lax.rem(col + d + cols, cols),
        )

    def sends_basis(d):
        return (holder == col) & (col + d >= 0) & (col + d < cols)

    @pl.when(col == 0)
    def _():
        factor_ref[...] = factor_in[...]
        for j in range(red // BLK):
            send_factor(j).start()
        row_products()

    for d in range(-parent_reach, parent_reach + 1):
        if d:
            @pl.when(sends_basis(d))
            def _():
                send_basis(d).start()

    def forward_factor():
        for j in range(red // BLK):
            send_factor(j).wait_recv()
            send_factor(j).start()

    @pl.when((col == 1) & (col < cols - 1))
    def _():
        forward_factor()

    for k in range(CHUNKS):
        @pl.when(relays())
        def _():
            remote(
                chunk(REACH, k), chunk(REACH + 2 * toward, k), row_send.at[0, k],
                row_recv.at[REACH + 2 * toward, k], row + toward, col,
            ).wait_recv()
            relay(k).start()

    for k in range(CHUNKS):
        for d in offsets:
            waiting = valid(d) if d % 2 else valid(d) & (2 * toward != d)

            @pl.when(waiting)
            def _():
                to_row(-d, k).wait_recv()

    own = [list_ref[0, col * entries + e] for e in range(entries)]
    leads = []
    for e in range(entries):
        seen = jnp.int32(0)
        for k in range(list_ref.shape[1]):
            same = (list_ref[0, k] == own[e]).astype(jnp.int32)
            before = (k < col * entries + e).astype(jnp.int32)
            seen = jnp.maximum(seen, same * before)
        leads.append(jnp.where(seen == 0, own[e], -1))
    tiles = []
    for e in range(entries):
        slot = jnp.clip(own[e] - row + REACH, 0, 2 * REACH)
        tiles.append(mm(products[e], table[slot], NN))
    zero = jnp.zeros((SKEL, SKEL), F32)
    for t in range(2 * cols):
        total = zero
        for e in range(entries):
            total = total + jnp.where(leads[e] == t, tiles[e], zero)
        outgoing[t // 2, :, (t % 2) * SKEL : (t % 2 + 1) * SKEL] = total

    def send_tile(d):
        other = lax.rem(col + d, cols)
        return remote(
            outgoing.at[other], incoming.at[d], tile_send.at[d], tile_recv.at[d], row, other
        )

    def wanted(c):
        return (holder + parent_reach >= c) & (holder <= c + parent_reach)

    for d in range(1, cols):
        @pl.when(wanted(lax.rem(col + d, cols)))
        def _():
            send_tile(d).start()

    @pl.when((col > 1) & (col < cols - 1))
    def _():
        forward_factor()

    total = outgoing[col]
    for d in range(1, cols):
        @pl.when(wanted(col))
        def _():
            send_tile(d).wait_recv()

        total = total + incoming[d]
    strip_ref[...] = total
    merged_ref[parity] = total

    to_pair = remote(
        strip_ref, merged_ref.at[parity], pair_send, pair_recv, row + 1 - 2 * parity, col
    )
    to_pair.start()

    def to_diag(d):
        return remote(
            strip_ref, diag_ref.at[parity], diag_send.at[d + reach_rows],
            diag_recv.at[parity], lax.rem(row + d + rows, rows), col,
        )

    def sends_diag(d):
        other = row + d
        near = ((other + 2 * parent_reach) // 2 >= col) & (other // 2 <= col + parent_reach)
        return (holder == col) & valid(d) & near & ((d % 2 == 0) | (toward == d))

    @pl.when(holder == col)
    def _():
        diag_ref[parity] = total

    for d in (-2, -1, 1, 2):
        @pl.when(sends_diag(d))
        def _():
            to_diag(d).start()

    remote(
        strip_ref, merged_ref.at[1 - parity], pair_send, pair_recv, row + 1 - 2 * parity, col
    ).wait_recv()
    inside = (holder + parent_reach >= col) & (holder <= col + parent_reach)

    def from_diag(s):
        return remote(
            diag_ref.at[s], diag_ref.at[s], diag_send.at[0], diag_recv.at[s], row + toward, col
        )

    @pl.when(inside & (holder != col))
    def _():
        from_diag(parity).wait_recv()
        from_diag(parity).start()

    @pl.when(inside)
    def _():
        from_diag(1 - parity).wait_recv()

    @pl.when((col == cols - 1) & (col > 0))
    def _():
        for j in range(red // BLK):
            send_factor(j).wait_recv()

    for d in range(-parent_reach, parent_reach + 1):
        if d:
            @pl.when(holder + d == col)
            def _():
                send_basis(d).wait_recv()

            @pl.when(sends_basis(d))
            def _():
                send_basis(d).wait_send()

    @pl.when(inside & (holder != col))
    def _():
        from_diag(parity).wait_send()

    to_pair.wait_send()
    for d in (-2, -1, 1, 2):
        @pl.when(sends_diag(d))
        def _():
            to_diag(d).wait_send()
    for d in range(1, cols):
        @pl.when(wanted(lax.rem(col + d, cols)))
        def _():
            send_tile(d).wait_send()

    for k in range(CHUNKS):
        @pl.when(col < cols - 1)
        def _():
            chain(k).wait_send()

        for d in offsets:
            @pl.when(direct(d))
            def _():
                to_row(d, k).wait_send()

        @pl.when(relays())
        def _():
            relay(k).wait_send()

    @pl.when(col < cols - 1)
    def _():
        for j in range(red // BLK):
            send_factor(j).wait_send()


def exchange(near_row, near, basis, upper_basis, combined, factor):
    rows, cols = lax.axis_size("row"), lax.axis_size("col")
    order = combined.shape[0]
    red = factor.shape[0]
    entries = near.shape[0]
    reach_rows = 2 * ((REACH + 1) // 2) + 1
    spans = 2 * REACH + 1
    vmem = pl.BlockSpec(memory_space=pltpu.VMEM)
    smem = pl.BlockSpec(memory_space=pltpu.SMEM)
    dma = pltpu.SemaphoreType.DMA
    return pl.pallas_call(
        functools.partial(exchange_kernel, rows, cols),
        out_shape=(
            jax.ShapeDtypeStruct((red, red), F32),
            jax.ShapeDtypeStruct((2, SKEL, 2 * SKEL), F32),
            jax.ShapeDtypeStruct((2, SKEL, 2 * SKEL), F32),
            jax.ShapeDtypeStruct((SKEL, 2 * SKEL), F32),
            jax.ShapeDtypeStruct((2 * SKEL, SKEL), F32),
        ),
        in_specs=[smem, pl.BlockSpec(memory_space=pl.ANY), vmem, vmem, vmem, vmem],
        out_specs=[vmem] * 5,
        scratch_shapes=[
            pltpu.VMEM(near.shape, F32),
            pltpu.VMEM((2 * SKEL, SKEL), F32),
            pltpu.VMEM((spans, order, SKEL), F32),
            pltpu.VMEM((entries, SKEL, order), F32),
            pltpu.VMEM((cols, SKEL, 2 * SKEL), F32),
            pltpu.VMEM((cols, SKEL, 2 * SKEL), F32),
            dma((CHUNKS,)), dma((CHUNKS,)),
            dma((spans, CHUNKS)), dma((spans, CHUNKS)),
            dma((red // BLK,)), dma((red // BLK,)),
            dma((cols,)), dma((cols,)),
            dma, dma,
            dma((2 * reach_rows + 1,)), dma((2,)),
            dma((entries,)), dma((2 * ((REACH + 1) // 2) + 1,)), dma,
        ],
        compiler_params=pltpu.CompilerParams(
            collective_id=0, has_side_effects=True, vmem_limit_bytes=40 * 1024 * 1024
        ),
        name="exchange",
    )(near_row, near, basis, upper_basis, combined, factor)


def parent_kernel(merged_ref, diag_ref, row_basis, col_basis, out_ref, work):
    basis = col_basis[...]
    pivot_block = mm(basis, mm(diag_ref[...], basis, NN), TN)
    rotated = mm(row_basis[...], mm(merged_ref[...], basis, NN), TN)
    row = lax.broadcasted_iota(jnp.int32, (BLK, BLK), 0)
    eye = jnp.where(row == lax.broadcasted_iota(jnp.int32, (BLK, BLK), 1), 1.0, 0.0)
    inside = jnp.abs(lax.axis_index("row") // 2 - lax.axis_index("col")) <= (REACH + 1) // 2
    load_block(work, jnp.where(inside, pivot_block[:SKEL, :SKEL], eye))
    chol_inv(work)
    inverse = work[:, BLK:]
    folded = mm(inverse, mm(inverse, pivot_block[:SKEL, SKEL:], NN), TN)
    full = rotated[:, SKEL:] - mm(rotated[:, :SKEL], folded, NN)
    half = SKEL // 2
    out_ref[...] = jnp.where(lax.axis_index("row") % 2 == 0, full[:half], full[half:])


def parent(merged, diag, row_basis, col_basis):
    return pl.pallas_call(
        parent_kernel,
        out_shape=jax.ShapeDtypeStruct((SKEL // 2, SKEL), F32),
        in_specs=[pl.BlockSpec(memory_space=pltpu.VMEM)] * 4,
        out_specs=pl.BlockSpec(memory_space=pltpu.VMEM),
        scratch_shapes=[pltpu.VMEM((BLK, 2 * BLK), F32)],
        name="parent",
    )(merged, diag, row_basis, col_basis)


def local(near_blocks, leaf_bases, upper_bases, near_list):
    order = leaf_bases.shape[1]
    red = order - SKEL
    near, basis, upper_basis = near_blocks[0], leaf_bases[0], upper_bases[0]

    def blank_pivot(near, basis):
        return jnp.zeros((red, red), F32), jnp.zeros((order, SKEL), F32)

    factor, combined = lax.cond(lax.axis_index("col") == 0, pivot, blank_pivot, near, basis)
    factor, merged, diag, strip, row_basis = exchange(
        near_list, near, basis, upper_basis, combined, factor
    )
    upper_half = parent(
        merged.reshape(2 * SKEL, 2 * SKEL), diag.reshape(2 * SKEL, 2 * SKEL), row_basis, upper_basis
    )
    return (factor, strip, upper_half)


def solution(mesh):
    return jax.shard_map(
        local,
        mesh=mesh,
        in_specs=(
            P("row", "col", None, None),
            P("row", None, None),
            P("col", None, None),
            P("row", None),
        ),
        out_specs=(P("row", None), P("row", "col"), P("row", "col")),
        check_vma=False,
    )
```
